256 devices in a mesh: chan: 16 (over z_lo, y), freq: 16 (over z_hi, x, core).
Axes of the slice: x: 4, y: 4, z: 8 (z_hi: 2, z_lo: 4; z = z_hi * 4 + z_lo), core: 2. Of those that a mesh axis runs over, the one named last changes fastest.
Arguments:
- traces: bfloat16 [64, 2048, 2048], P('freq', 'chan'), may hold values from -6 to 6
Outputs:
- correlations: bfloat16 [64, 2048, 2048], P('freq', 'chan')
The draws below stay inside these ranges and needn't reach their ends.
All inputs are finite; a program needn't handle non-finite values.
Results may differ from the reference program's by a relative error of at most 0.0076.
Values may be sent and summed in bfloat16 or wider, within the bound.
A program may use at most 128 MiB of HBM per device.

```python
import math
import jax
import jax.numpy as jnp
from jax import lax

S = 2048
F = 1024
K = 64
C = 2048
W = 64


def block_scale(own_key, extent, split, low, high):
    level = 1.0
    for dim, blocks in split:
        draws = jax.random.uniform(jax.random.fold_in(jax.random.fold_in(own_key, 6), dim), (blocks,), jnp.float32, low / len(split), high / len(split))
        level = level * jnp.repeat(jnp.exp(draws), extent[dim] // blocks).reshape((-1,) + (1,) * (len(extent) - 1 - dim))
    return level


def bell_draw(stream_key, shape, scale, limit, shards=(), kind=jnp.bfloat16):
    factor_of = block_scale(stream_key, shape, shards, -0.22, 0.18) if shards else 1.0
    array = jax.random.normal(stream_key, shape, jnp.float32) * scale * factor_of
    return jnp.minimum(jnp.maximum(array, -limit), limit).astype(kind)


def setup_inputs(seed: int = 0) -> dict:
    arg_keys = jax.random.split(jax.random.key(seed), 2)
    return {
        "traces": bell_draw(arg_keys[0], (W, C, S), 1.0, 6.0, ((0, 16), (1, 16))),
    }


def forward_tables():
    sample_idx = jnp.arange(S, dtype=jnp.int32)
    freq_idx = jnp.arange(F, dtype=jnp.int32)
    phases = sample_idx[:, None] * freq_idx[None, :] % S
    angles = 2.0 * math.pi / S * phases.astype(jnp.float32)
    return (jnp.cos(angles).astype(jnp.bfloat16), (-jnp.sin(angles)).astype(jnp.bfloat16))

def inverse_tables():
    freq_idx = jnp.arange(F, dtype=jnp.int32)
    lag_idx = jnp.arange(S, dtype=jnp.int32) - S // 2
    phases = jnp.mod(freq_idx[:, None] * lag_idx[None, :], S)
    angles = 2.0 * math.pi / S * phases.astype(jnp.float32)
    factor = 1.0 / math.sqrt(F)
    return ((jnp.cos(angles) * factor).astype(jnp.bfloat16), (-jnp.sin(angles) * factor).astype(jnp.bfloat16))

def reference(traces):
    cos_table, sin_table = forward_tables()

    def whiten(window):
        real_part = jnp.dot(window, cos_table, preferred_element_type=jnp.float32)
        imag_part = jnp.dot(window, sin_table, preferred_element_type=jnp.float32)
        energy = real_part * real_part + imag_part * imag_part
        water_level = 0.1 * lax.optimization_barrier(jnp.mean(energy, axis=1, keepdims=True))
        inverse_norm = 1.0 / jnp.sqrt(energy + water_level + 1e-06)
        return ((real_part * inverse_norm).astype(jnp.bfloat16), (imag_part * inverse_norm).astype(jnp.bfloat16))
    white_real, white_imag = lax.map(whiten, traces)
    padded_real = jnp.pad(white_real, ((0, 0), (0, K), (0, 0)))
    padded_imag = jnp.pad(white_imag, ((0, 0), (0, K), (0, 0)))
    norm_factor = 1.0 / math.sqrt(W)

    def cross(offset):
        other_real = lax.dynamic_slice_in_dim(padded_real, offset, C, axis=1).astype(jnp.float32)
        other_imag = lax.dynamic_slice_in_dim(padded_imag, offset, C, axis=1).astype(jnp.float32)
        own_real = white_real.astype(jnp.float32)
        own_imag = white_imag.astype(jnp.float32)
        sum_real = lax.optimization_barrier(jnp.sum(own_real * other_real + own_imag * other_imag, axis=0))
        sum_imag = lax.optimization_barrier(jnp.sum(own_imag * other_real - own_real * other_imag, axis=0))
        return ((sum_real * norm_factor).astype(jnp.bfloat16), (sum_imag * norm_factor).astype(jnp.bfloat16))
    stacked_real, stacked_imag = lax.map(cross, jnp.arange(1, K + 1, dtype=jnp.int32))
    inv_cos, inv_sin = inverse_tables()
    result = jnp.dot(stacked_real.reshape(K * C, F), inv_cos, preferred_element_type=jnp.float32)
    result = result + jnp.dot(stacked_imag.reshape(K * C, F), inv_sin, preferred_element_type=jnp.float32)
    return result.reshape(K, C, S).astype(jnp.bfloat16)
```

```python
import functools
import math

import jax
import jax.numpy as jnp
import ml_dtypes
import numpy as np
from jax import lax
from jax.experimental import pallas as pl
from jax.experimental.pallas import tpu as pltpu
from jax.sharding import PartitionSpec as P

MESH = pl.DeviceIdType.MESH
BF16 = jnp.bfloat16
F32 = jnp.float32

S = 2048
W4 = 4
N = 16
CB = 128
K = 64
STAGES = 4
FS = 64 // STAGES
GS = FS // 4
ROWS = N * 2 * FS


def table():
    stage, shard, local = np.meshgrid(np.arange(STAGES), np.arange(N), np.arange(FS), indexing="ij")
    freq = (shard * 64 + stage * FS + local)[:, :, None, :, None]
    angle = (2.0 * math.pi / S) * ((freq * np.arange(S)) % S)
    values = np.concatenate([np.cos(angle), -np.sin(angle)], axis=2)
    return values.reshape(STAGES, ROWS, S).astype(ml_dtypes.bfloat16)


def partner(me, d):
    half, x, core = me // 8, (me // 2) % 4, me % 2
    half = (half + 1 - d // 8) % 2
    x = (x + 1 + (d % 8) // 2) % 4
    core = (core + 1 + d) % 2
    return half * 8 + x * 2 + core


def kernel(
    x_hbm, tbl_hbm, o_hbm,
    x_v, tbl, sums, level, spec, mix, send1, recv1, hsend, hrecv, gram, zbuf, send2, recv2, lhs2, acc, out_v,
    x_sem, tbl_sem, s1_sem, r1_sem, l1_sem, hs_sem, hr_sem, s2_sem, r2_sem, l2_sem, o_sem,
):
    chan, me = lax.axis_index("chan"), lax.axis_index("freq")

    x_copy = pltpu.make_async_copy(x_hbm, x_v, x_sem)
    x_copy.start()
    tbl_copies = [pltpu.make_async_copy(tbl_hbm.at[s], tbl.at[s], tbl_sem.at[s]) for s in range(STAGES)]
    for copy in tbl_copies:
        copy.start()

    barrier = pltpu.get_barrier_semaphore()
    for d in range(N - 1):
        pl.semaphore_signal(barrier, inc=1, device_id=(chan, partner(me, d)), device_id_type=MESH)

    @pl.when(chan < N - 1)
    def _():
        pl.semaphore_signal(barrier, inc=1, device_id=(chan + 1, me), device_id_type=MESH)

    x_copy.wait()

    def fold(b, carry):
        rows = pl.ds(pl.multiple_of(b * 64, 64), 64)
        squares = jnp.zeros((64, 128), F32)
        plain = jnp.zeros((64, 128), F32)
        for i in range(S // 128):
            part = x_v[rows, i * 128 : (i + 1) * 128].astype(F32)
            squares += part * part
            plain += part
        sums[rows, 0:128] = squares
        sums[rows, 128:256] = plain
        return carry

    lax.fori_loop(0, W4 * CB // 64, fold, 0)
    odd = lax.broadcasted_iota(jnp.int32, (128, 128), 0) % 2
    for w in range(W4):
        squares = jnp.transpose(sums[w * CB : (w + 1) * CB, 0:128])
        plain = jnp.transpose(sums[w * CB : (w + 1) * CB, 128:256])
        even_sum = jnp.sum(jnp.where(odd == 0, plain, 0.0), axis=0, keepdims=True)
        odd_sum = jnp.sum(jnp.where(odd == 1, plain, 0.0), axis=0, keepdims=True)
        mean = jnp.sum(squares, axis=0, keepdims=True) + even_sum * odd_sum * (1.0 / 512)
        mean = 0.1 * jnp.maximum(mean, 0.0) + 1e-6
        level[:, w * CB : (w + 1) * CB] = jnp.broadcast_to(mean, (8, CB))

    pl.semaphore_wait(barrier, jnp.where(chan > 0, N, N - 1))

    def first(s, d):
        p = partner(me, d)
        return pltpu.make_async_remote_copy(
            src_ref=send1.at[s, p], dst_ref=recv1.at[s, :, :, me], send_sem=s1_sem.at[s, d], recv_sem=r1_sem.at[s, d],
            device_id=(chan, p), device_id_type=MESH,
        )

    def first_own(s):
        return pltpu.make_async_copy(send1.at[s, me], recv1.at[s, :, :, me], l1_sem.at[s])

    def rim(s):
        return pltpu.make_async_remote_copy(
            src_ref=hsend.at[s], dst_ref=hrecv.at[s], send_sem=hs_sem.at[s], recv_sem=hr_sem.at[s],
            device_id=(chan - 1, me), device_id_type=MESH,
        )

    def second(s, d):
        p = partner(me, d)
        return pltpu.make_async_remote_copy(
            src_ref=send2.at[s, p], dst_ref=recv2.at[s, :, me], send_sem=s2_sem.at[s, d], recv_sem=r2_sem.at[s, d],
            device_id=(chan, p), device_id_type=MESH,
        )

    def second_own(s):
        return pltpu.make_async_copy(send2.at[s, me], recv2.at[s, :, me], l2_sem.at[s])

    def spectra(s, carry):
        pltpu.make_async_copy(tbl_hbm.at[s], tbl.at[s], tbl_sem.at[s]).wait()
        spec[...] = lax.dot_general(
            tbl[s], x_v[...], (((1,), (1,)), ((), ())), preferred_element_type=F32
        ).reshape(N, 2, FS, W4 * CB)

        def whiten(d, carry):
            p = partner(me, d)
            real, imag = spec[p, 0], spec[p, 1]
            scale = lax.rsqrt(real * real + imag * imag + level[0:1, :])
            for part, value in enumerate((real * scale, imag * scale)):
                for w in range(W4):
                    mix[pl.ds(part * 4 * FS + w, FS, stride=4), :] = value[:, w * CB : (w + 1) * CB]
            for part in range(2):
                rows = mix[part * 4 * FS : (part + 1) * 4 * FS, :]
                send1[s, p, part] = rows.astype(BF16).reshape(GS, 16, CB)

            @pl.when(d < N - 1)
            def _():
                first(s, d).start()

            return carry

        lax.fori_loop(0, N, whiten, 0)
        first_own(s).start()
        return carry

    lax.fori_loop(0, STAGES, spectra, 0)

    @pl.when(chan == N - 1)
    def _():
        hrecv[...] = jnp.zeros_like(hrecv)

    lane = lax.broadcasted_iota(jnp.int32, (8, CB), 1)
    shift = lane + 1
    sublane = lax.broadcasted_iota(jnp.int32, (8, CB), 0)
    in_own = (sublane + shift % 8) < 8

    def pick(bit, far, near):
        rows = near.shape[0]
        mask = (shift // bit) % 2 == 1
        return jnp.where(mask[None], far.reshape(rows // 8, 8, CB), near.reshape(rows // 8, 8, CB)).reshape(rows, CB)

    def skew(g):
        g = jnp.concatenate([pick(128, g[128:192], g[0:64]), g[64:192]], axis=0)
        g = pick(64, g[64:192], g[0:128])
        g = pick(32, g[32:128], g[0:96])
        g = pick(16, g[16:96], g[0:80])
        g = pick(8, g[8:80], g[0:72])
        g = g.reshape(9, 8, CB)
        for bit in (4, 2, 1):
            mask = (shift // bit) % 2 == 1
            g = jnp.where(mask[None], pltpu.roll(g, 8 - bit, axis=1), g)
        return jnp.where(in_own[None], g[0:8], g[1:9]).reshape(64, CB)

    def middle(s, carry):
        for d in range(N - 1):
            first(s, d).wait_recv()
        first_own(s).wait()

        def pack(g, carry):
            left = recv1[s, 0, g].reshape(N * 16, CB)[:, 0:64]
            right = recv1[s, 1, g].reshape(N * 16, CB)[:, 0:64]
            hsend[s, g] = jnp.concatenate([left, right], axis=1)
            return carry

        lax.fori_loop(0, GS, pack, 0)

        @pl.when(chan > 0)
        def _():
            rim(s).start()

        @pl.when(chan < N - 1)
        def _():
            rim(s).wait_recv()

        def group(g, carry):
            real = recv1[s, 0, g].reshape(N * 16, CB)
            imag = recv1[s, 1, g].reshape(N * 16, CB)
            rim_t = jnp.transpose(hrecv[s, g])
            real_t = jnp.concatenate([jnp.transpose(real), rim_t[0:64]], axis=0)
            imag_t = jnp.concatenate([jnp.transpose(imag), rim_t[64:128]], axis=0)
            right = jnp.concatenate(
                [jnp.concatenate([real, imag], axis=1), jnp.concatenate([imag, -real], axis=1)], axis=0
            )
            left = jnp.concatenate([real_t, imag_t], axis=1)
            which = (lax.broadcasted_iota(jnp.int32, left.shape, 1) % 16) // 4
            for f in range(4):
                gram[f * 192 : (f + 1) * 192, :] = jnp.dot(
                    jnp.where(which == f, left, jnp.zeros_like(left)), right, preferred_element_type=F32
                )
            for f in range(4):
                for part in range(2):
                    zbuf[pl.ds(part * FS + g * 4 + f, K, stride=2 * FS), :] = skew(
                        gram[f * 192 : (f + 1) * 192, part * CB : (part + 1) * CB]
                    )
            return carry

        lax.fori_loop(0, GS, group, 0)

        parity = lax.broadcasted_iota(jnp.int32, (4 * 2 * FS, CB), 0) % 2
        sign = jnp.where(parity == 0, 1.0 / 256, -1.0 / 256)

        def give(d, carry):
            p = partner(me, d)
            rows = zbuf[pl.ds(pl.multiple_of(p * 8 * FS, 8 * FS), 8 * FS), :]
            send2[s, p] = (rows * sign).astype(BF16).reshape(4, 2 * FS, CB)

            @pl.when(d < N - 1)
            def _():
                second(s, d).start()

            return carry

        lax.fori_loop(0, N, give, 0)
        second_own(s).start()
        return carry

    lax.fori_loop(0, STAGES, middle, 0)

    def lags(s):
        for d in range(N - 1):
            second(s, d).wait_recv()
        second_own(s).wait()
        for k in range(4):
            lhs2[k * CB : (k + 1) * CB, :] = jnp.transpose(recv2[s, k].reshape(ROWS, CB))

        def tile(t, carry):
            columns = pl.ds(pl.multiple_of(t * 512, 512), 512)
            product = jnp.dot(lhs2[...], tbl[s, :, columns], preferred_element_type=F32)
            if s == 0:
                acc[t] = product
            elif s < STAGES - 1:
                acc[t] += product
            else:
                out_v[t] = (acc[t] + product).astype(BF16)
                pltpu.make_async_copy(out_v.at[t], o_hbm.at[:, columns], o_sem.at[t]).start()
            return carry

        lax.fori_loop(0, 4, tile, 0)

    for s in range(STAGES):
        lags(s)

    for s in range(STAGES):
        for d in range(N - 1):
            first(s, d).wait_send()
            second(s, d).wait_send()

        @pl.when(chan > 0)
        def _():
            rim(s).wait_send()

    for t in range(4):
        pltpu.make_async_copy(out_v.at[t], o_hbm.at[:, t * 512 : (t + 1) * 512], o_sem.at[t]).wait()


def per_device(traces, tbl):
    rows = W4 * CB
    dma = pltpu.SemaphoreType.DMA
    any_space = pl.BlockSpec(memory_space=pl.ANY)
    out = pl.pallas_call(
        kernel,
        out_shape=jax.ShapeDtypeStruct((rows, S), BF16),
        in_specs=[any_space, any_space],
        out_specs=any_space,
        scratch_shapes=[
            pltpu.VMEM((rows, S), BF16),
            pltpu.VMEM((STAGES, ROWS, S), BF16),
            pltpu.VMEM((rows, 256), F32),
            pltpu.VMEM((8, rows), F32),
            pltpu.VMEM((N, 2, FS, rows), F32),
            pltpu.VMEM((2 * 4 * FS, CB), F32),
            pltpu.VMEM((STAGES, N, 2, GS, 16, CB), BF16),
            pltpu.VMEM((STAGES, 2, GS, N, 16, CB), BF16),
            pltpu.VMEM((STAGES, GS, N * 16, CB), BF16),
            pltpu.VMEM((STAGES, GS, N * 16, CB), BF16),
            pltpu.VMEM((4 * 192, 256), F32),
            pltpu.VMEM((K * 2 * FS, CB), F32),
            pltpu.VMEM((STAGES, N, 4, 2 * FS, CB), BF16),
            pltpu.VMEM((STAGES, 4, N, 2 * FS, CB), BF16),
            pltpu.VMEM((4 * CB, ROWS), BF16),
            pltpu.VMEM((4, rows, 512), F32),
            pltpu.VMEM((4, rows, 512), BF16),
            dma, dma((STAGES,)),
            dma((STAGES, N)), dma((STAGES, N)), dma((STAGES,)),
            dma((STAGES,)), dma((STAGES,)),
            dma((STAGES, N)), dma((STAGES, N)), dma((STAGES,)),
            dma((4,)),
        ],
        compiler_params=pltpu.CompilerParams(collective_id=0, has_side_effects=True, vmem_limit_bytes=56 * 2**20),
        name="correlate",
    )(traces.reshape(rows, S), tbl)
    return out.reshape(traces.shape)


def solution(mesh):
    placed = P("freq", "chan", None)
    mapped = jax.shard_map(per_device, mesh=mesh, in_specs=(placed, P()), out_specs=placed, check_vma=False)
    return lambda traces: mapped(traces, jnp.asarray(table()))
```

```python
import functools
import math

import jax
import jax.numpy as jnp
import ml_dtypes
import numpy as np
from jax import lax
from jax.experimental import pallas as pl
from jax.experimental.pallas import tpu as pltpu
from jax.sharding import PartitionSpec as P

MESH = pl.DeviceIdType.MESH
BF16 = jnp.bfloat16
F32 = jnp.float32

S = 2048
W4 = 4
N = 16
CB = 128
K = 64
STAGES = 4
FS = 64 // STAGES
GS = FS // 4
ROWS = N * 2 * FS


def table():
    stage, shard, local = np.meshgrid(np.arange(STAGES), np.arange(N), np.arange(FS), indexing="ij")
    freq = (shard * 64 + stage * FS + local)[:, :, None, :, None]
    angle = (2.0 * math.pi / S) * ((freq * np.arange(S)) % S)
    values = np.concatenate([np.cos(angle), -np.sin(angle)], axis=2)
    return values.reshape(STAGES, ROWS, S).astype(ml_dtypes.bfloat16)


def partner(me, d):
    half, x, core = me // 8, (me // 2) % 4, me % 2
    half = (half + 1 - d // 8) % 2
    x = (x + 1 + (d % 8) // 2) % 4
    core = (core + 1 + d) % 2
    return half * 8 + x * 2 + core


def kernel(
    x_hbm, tbl_hbm, o_ref,
    x_v, tbl, sums, level, spec, mix, send1, recv1, hsend, hrecv, passing, gram, zbuf, send2, recv2, lhs2, acc,
    x_sem, tbl_sem, s1_sem, r1_sem, l1_sem, hs_sem, hr_sem, ps_sem, pr_sem, s2_sem, r2_sem, l2_sem,
):
    chan, me = lax.axis_index("chan"), lax.axis_index("freq")
    depth, y = chan // 4, chan % 4
    crossing = (y == 0) & (depth > 0)
    relaying = (y > 0) & (depth > 0)
    crossed = (y == 3) & (depth < 3)

    x_copy = pltpu.make_async_copy(x_hbm, x_v, x_sem)
    x_copy.start()
    tbl_copies = [pltpu.make_async_copy(tbl_hbm.at[s], tbl.at[s], tbl_sem.at[s]) for s in range(STAGES)]
    for copy in tbl_copies:
        copy.start()

    barrier = pltpu.get_barrier_semaphore()
    for d in range(N - 1):
        pl.semaphore_signal(barrier, inc=1, device_id=(chan, partner(me, d)), device_id_type=MESH)

    @pl.when(chan < N - 1)
    def _():
        pl.semaphore_signal(barrier, inc=1, device_id=(chan + 1, me), device_id_type=MESH)

    @pl.when(crossed)
    def _():
        for g in range(1, 4):
            pl.semaphore_signal(barrier, inc=1, device_id=(chan + 1 + g, me), device_id_type=MESH)

    @pl.when(relaying)
    def _():
        pl.semaphore_signal(barrier, inc=1, device_id=(chan - y, me), device_id_type=MESH)

    x_copy.wait()

    def fold(b, carry):
        rows = pl.ds(pl.multiple_of(b * 64, 64), 64)
        squares = jnp.zeros((64, 128), F32)
        plain = jnp.zeros((64, 128), F32)
        for i in range(S // 128):
            part = x_v[rows, i * 128 : (i + 1) * 128].astype(F32)
            squares += part * part
            plain += part
        sums[rows, 0:128] = squares
        sums[rows, 128:256] = plain
        return carry

    lax.fori_loop(0, W4 * CB // 64, fold, 0)
    odd = lax.broadcasted_iota(jnp.int32, (128, 128), 0) % 2
    for w in range(W4):
        squares = jnp.transpose(sums[w * CB : (w + 1) * CB, 0:128])
        plain = jnp.transpose(sums[w * CB : (w + 1) * CB, 128:256])
        even_sum = jnp.sum(jnp.where(odd == 0, plain, 0.0), axis=0, keepdims=True)
        odd_sum = jnp.sum(jnp.where(odd == 1, plain, 0.0), axis=0, keepdims=True)
        mean = jnp.sum(squares, axis=0, keepdims=True) + even_sum * odd_sum * (1.0 / 512)
        mean = 0.1 * jnp.maximum(mean, 0.0) + 1e-6
        level[:, w * CB : (w + 1) * CB] = jnp.broadcast_to(mean, (8, CB))

    greeted = N - 1 + jnp.where(chan > 0, 1, 0) + jnp.where(crossing, 3, 0) + jnp.where(relaying, 1, 0)
    pl.semaphore_wait(barrier, greeted)

    def first(s, d):
        p = partner(me, d)
        return pltpu.make_async_remote_copy(
            src_ref=send1.at[s, p], dst_ref=recv1.at[s, :, :, me], send_sem=s1_sem.at[s, d], recv_sem=r1_sem.at[s, d],
            device_id=(chan, p), device_id_type=MESH,
        )

    def first_own(s):
        return pltpu.make_async_copy(send1.at[s, me], recv1.at[s, :, :, me], l1_sem.at[s])

    def rim(s, g):
        return pltpu.make_async_remote_copy(
            src_ref=hsend.at[s, g], dst_ref=hrecv.at[s, g], send_sem=hs_sem.at[s, g], recv_sem=hr_sem.at[s, g],
            device_id=(chan - 1, me), device_id_type=MESH,
        )

    def to_relay(s, g):
        return pltpu.make_async_remote_copy(
            src_ref=hsend.at[s, g], dst_ref=passing.at[s], send_sem=hs_sem.at[s, g], recv_sem=pr_sem.at[s],
            device_id=(chan + g, me), device_id_type=MESH,
        )

    def from_relay(s):
        return pltpu.make_async_remote_copy(
            src_ref=passing.at[s], dst_ref=hrecv.at[s, y], send_sem=ps_sem.at[s], recv_sem=hr_sem.at[s, y],
            device_id=(chan - y - 1, me), device_id_type=MESH,
        )

    def second(s, d):
        p = partner(me, d)
        return pltpu.make_async_remote_copy(
            src_ref=send2.at[s, p], dst_ref=recv2.at[s, :, me], send_sem=s2_sem.at[s, d], recv_sem=r2_sem.at[s, d],
            device_id=(chan, p), device_id_type=MESH,
        )

    def second_own(s):
        return pltpu.make_async_copy(send2.at[s, me], recv2.at[s, :, me], l2_sem.at[s])

    def spectra(s, carry):
        pltpu.make_async_copy(tbl_hbm.at[s], tbl.at[s], tbl_sem.at[s]).wait()
        spec[...] = lax.dot_general(
            tbl[s], x_v[...], (((1,), (1,)), ((), ())), preferred_element_type=F32
        ).reshape(N, 2, FS, W4 * CB)

        def whiten(d, carry):
            p = partner(me, d)
            real, imag = spec[p, 0], spec[p, 1]
            scale = lax.rsqrt(real * real + imag * imag + level[0:1, :])
            for part, value in enumerate((real * scale, imag * scale)):
                for w in range(W4):
                    mix[pl.ds(part * 4 * FS + w, FS, stride=4), :] = value[:, w * CB : (w + 1) * CB]
            for part in range(2):
                rows = mix[part * 4 * FS : (part + 1) * 4 * FS, :]
                send1[s, p, part] = rows.astype(BF16).reshape(GS, 16, CB)

            @pl.when(d < N - 1)
            def _():
                first(s, d).start()

            return carry

        lax.fori_loop(0, N, whiten, 0)
        first_own(s).start()
        return carry

    lax.fori_loop(0, STAGES, spectra, 0)

    @pl.when(chan == N - 1)
    def _():
        hrecv[...] = jnp.zeros_like(hrecv)

    lane = lax.broadcasted_iota(jnp.int32, (8, CB), 1)
    shift = lane + 1
    sublane = lax.broadcasted_iota(jnp.int32, (8, CB), 0)
    in_own = (sublane + shift % 8) < 8

    def pick(bit, far, near):
        rows = near.shape[0]
        mask = (shift // bit) % 2 == 1
        return jnp.where(mask[None], far.reshape(rows // 8, 8, CB), near.reshape(rows // 8, 8, CB)).reshape(rows, CB)

    def skew(g):
        g = jnp.concatenate([pick(128, g[128:192], g[0:64]), g[64:192]], axis=0)
        g = pick(64, g[64:192], g[0:128])
        g = pick(32, g[32:128], g[0:96])
        g = pick(16, g[16:96], g[0:80])
        g = pick(8, g[8:80], g[0:72])
        g = g.reshape(9, 8, CB)
        for bit in (4, 2, 1):
            mask = (shift // bit) % 2 == 1
            g = jnp.where(mask[None], pltpu.roll(g, 8 - bit, axis=1), g)
        return jnp.where(in_own[None], g[0:8], g[1:9]).reshape(64, CB)

    def gather(s):
        for d in range(N - 1):
            first(s, d).wait_recv()
        first_own(s).wait()

        def pack(g, carry):
            left = recv1[s, 0, g].reshape(N * 16, CB)[:, 0:64]
            right = recv1[s, 1, g].reshape(N * 16, CB)[:, 0:64]
            hsend[s, g] = jnp.concatenate([left, right], axis=1)
            return carry

        lax.fori_loop(0, GS, pack, 0)

        @pl.when(chan > 0)
        def _():
            rim(s, 0).start()

        @pl.when(y > 0)
        def _():
            for g in range(1, GS):
                rim(s, g).start()

        @pl.when(crossing)
        def _():
            for g in range(1, GS):
                to_relay(s, g).start()

    def relay(s):
        @pl.when(relaying)
        def _():
            to_relay(s, 1).wait_recv()
            from_relay(s).start()

    def products(s):
        @pl.when(chan < N - 1)
        def _():
            for g in range(GS):
                rim(s, g).wait_recv()

        def group(g, carry):
            real = recv1[s, 0, g].reshape(N * 16, CB)
            imag = recv1[s, 1, g].reshape(N * 16, CB)
            rim_t = jnp.transpose(hrecv[s, g])
            real_t = jnp.concatenate([jnp.transpose(real), rim_t[0:64]], axis=0)
            imag_t = jnp.concatenate([jnp.transpose(imag), rim_t[64:128]], axis=0)
            right = jnp.concatenate(
                [jnp.concatenate([real, imag], axis=1), jnp.concatenate([imag, -real], axis=1)], axis=0
            )
            left = jnp.concatenate([real_t, imag_t], axis=1)
            which = (lax.broadcasted_iota(jnp.int32, left.shape, 1) % 16) // 4
            for f in range(4):
                gram[f * 192 : (f + 1) * 192, :] = jnp.dot(
                    jnp.where(which == f, left, jnp.zeros_like(left)), right, preferred_element_type=F32
                )
            for f in range(4):
                for part in range(2):
                    zbuf[pl.ds(part * FS + g * 4 + f, K, stride=2 * FS), :] = skew(
                        gram[f * 192 : (f + 1) * 192, part * CB : (part + 1) * CB]
                    )
            return carry

        lax.fori_loop(0, GS, group, 0)

        parity = lax.broadcasted_iota(jnp.int32, (4 * 2 * FS, CB), 0) % 2
        sign = jnp.where(parity == 0, 1.0 / 256, -1.0 / 256)

        def give(d, carry):
            p = partner(me, d)
            rows = zbuf[pl.ds(pl.multiple_of(p * 8 * FS, 8 * FS), 8 * FS), :]
            send2[s, p] = (rows * sign).astype(BF16).reshape(4, 2 * FS, CB)

            @pl.when(d < N - 1)
            def _():
                second(s, d).start()

            return carry

        lax.fori_loop(0, N, give, 0)
        second_own(s).start()

    gather(0)
    relay(0)

    def middle(s, carry):
        gather(s)
        relay(s)
        products(s - 1)
        return carry

    lax.fori_loop(1, STAGES, middle, 0)
    products(STAGES - 1)

    def lags(s):
        for d in range(N - 1):
            second(s, d).wait_recv()
        second_own(s).wait()
        for k in range(4):
            lhs2[k * CB : (k + 1) * CB, :] = jnp.transpose(recv2[s, k].reshape(ROWS, CB))

        def tile(t, carry):
            columns = pl.ds(pl.multiple_of(t * 512, 512), 512)
            product = jnp.dot(lhs2[...], tbl[s, :, columns], preferred_element_type=F32)
            if s == 0:
                acc[t] = product
            elif s < STAGES - 1:
                acc[t] += product
            else:
                o_ref[:, columns] = (acc[t] + product).astype(BF16)
            return carry

        lax.fori_loop(0, 4, tile, 0)

    for s in range(STAGES):
        lags(s)

    for s in range(STAGES):
        for d in range(N - 1):
            first(s, d).wait_send()
            second(s, d).wait_send()

        @pl.when(chan > 0)
        def _():
            for g in range(GS):
                rim(s, g).wait_send()

        @pl.when(relaying)
        def _():
            from_relay(s).wait_send()


def per_device(traces, tbl):
    rows = W4 * CB
    dma = pltpu.SemaphoreType.DMA
    any_space = pl.BlockSpec(memory_space=pltpu.HBM)
    out = pl.pallas_call(
        kernel,
        out_shape=pltpu.VMEM((rows, S), BF16),
        in_specs=[any_space, any_space],
        out_specs=pl.BlockSpec(memory_space=pltpu.VMEM),
        scratch_shapes=[
            pltpu.VMEM((rows, S), BF16),
            pltpu.VMEM((STAGES, ROWS, S), BF16),
            pltpu.VMEM((rows, 256), F32),
            pltpu.VMEM((8, rows), F32),
            pltpu.VMEM((N, 2, FS, rows), F32),
            pltpu.VMEM((2 * 4 * FS, CB), F32),
            pltpu.VMEM((STAGES, N, 2, GS, 16, CB), BF16),
            pltpu.VMEM((STAGES, 2, GS, N, 16, CB), BF16),
            pltpu.VMEM((STAGES, GS, N * 16, CB), BF16),
            pltpu.VMEM((STAGES, GS, N * 16, CB), BF16),
            pltpu.VMEM((STAGES, N * 16, CB), BF16),
            pltpu.VMEM((4 * 192, 256), F32),
            pltpu.VMEM((K * 2 * FS, CB), F32),
            pltpu.VMEM((STAGES, N, 4, 2 * FS, CB), BF16),
            pltpu.VMEM((STAGES, 4, N, 2 * FS, CB), BF16),
            pltpu.VMEM((4 * CB, ROWS), BF16),
            pltpu.VMEM((4, rows, 512), F32),
            dma, dma((STAGES,)),
            dma((STAGES, N)), dma((STAGES, N)), dma((STAGES,)),
            dma((STAGES, GS)), dma((STAGES, GS)), dma((STAGES,)), dma((STAGES,)),
            dma((STAGES, N)), dma((STAGES, N)), dma((STAGES,)),
        ],
        compiler_params=pltpu.CompilerParams(collective_id=0, has_side_effects=True, vmem_limit_bytes=60 * 2**20),
        name="correlate",
    )(traces.reshape(rows, S), tbl)
    return out.reshape(traces.shape)


def solution(mesh):
    placed = P("freq", "chan", None)
    mapped = jax.shard_map(per_device, mesh=mesh, in_specs=(placed, P()), out_specs=placed, check_vma=False)
    return lambda traces: mapped(traces, jnp.asarray(table()))
```

```python
import functools
import math

import jax
import jax.numpy as jnp
import ml_dtypes
import numpy as np
from jax import lax
from jax.experimental import pallas as pl
from jax.experimental.pallas import tpu as pltpu
from jax.sharding import PartitionSpec as P

MESH = pl.DeviceIdType.MESH
BF16 = jnp.bfloat16
F32 = jnp.float32

S = 2048
W4 = 4
N = 16
CB = 128
K = 64
STAGES = 4
FS = 64 // STAGES
GS = FS // 4
ROWS = N * 2 * FS


def table():
    stage, shard, local = np.meshgrid(np.arange(STAGES), np.arange(N), np.arange(FS), indexing="ij")
    freq = (shard * 64 + stage * FS + local)[:, :, None, :, None]
    angle = (2.0 * math.pi / S) * ((freq * np.arange(S)) % S)
    values = np.concatenate([np.cos(angle), -np.sin(angle)], axis=2)
    return values.reshape(STAGES, ROWS, S).astype(ml_dtypes.bfloat16)


def partner(me, d):
    half, x, core = me // 8, (me // 2) % 4, me % 2
    half = (half + 1 - d // 8) % 2
    x = (x + 1 + (d % 8) // 2) % 4
    core = (core + 1 + d) % 2
    return half * 8 + x * 2 + core


def kernel(
    x_hbm, tbl_hbm, o_ref,
    x_v, tbl, sums, level, spec, mix, send1, recv1, hsend, hrecv, passing, gram, zbuf, send2, recv2, lhs2, acc,
    x_sem, tbl_sem, s1_sem, r1_sem, l1_sem, hs_sem, hr_sem, ps_sem, pr_sem, s2_sem, r2_sem, l2_sem,
):
    chan, me = lax.axis_index("chan"), lax.axis_index("freq")
    depth, y = chan // 4, chan % 4
    crossing = (y == 0) & (depth > 0)
    relaying = (y > 0) & (depth > 0)
    crossed = (y == 3) & (depth < 3)

    x_copy = pltpu.make_async_copy(x_hbm, x_v, x_sem)
    x_copy.start()
    tbl_copies = [pltpu.make_async_copy(tbl_hbm.at[s], tbl.at[s], tbl_sem.at[s]) for s in range(STAGES)]
    for copy in tbl_copies:
        copy.start()

    barrier = pltpu.get_barrier_semaphore()
    for d in range(N - 1):
        pl.semaphore_signal(barrier, inc=1, device_id=(chan, partner(me, d)), device_id_type=MESH)

    @pl.when(chan < N - 1)
    def _():
        pl.semaphore_signal(barrier, inc=1, device_id=(chan + 1, me), device_id_type=MESH)

    @pl.when(crossed)
    def _():
        for g in range(1, 4):
            pl.semaphore_signal(barrier, inc=1, device_id=(chan + 1 + g, me), device_id_type=MESH)

    @pl.when(relaying)
    def _():
        pl.semaphore_signal(barrier, inc=1, device_id=(chan - y, me), device_id_type=MESH)

    x_copy.wait()

    def fold(b, carry):
        rows = pl.ds(pl.multiple_of(b * 64, 64), 64)
        squares = jnp.zeros((64, 128), F32)
        plain = jnp.zeros((64, 128), F32)
        for i in range(S // 128):
            part = x_v[rows, i * 128 : (i + 1) * 128].astype(F32)
            squares += part * part
            plain += part
        sums[rows, 0:128] = squares
        sums[rows, 128:256] = plain
        return carry

    lax.fori_loop(0, W4 * CB // 64, fold, 0)
    odd = lax.broadcasted_iota(jnp.int32, (128, 128), 0) % 2
    for w in range(W4):
        squares = jnp.transpose(sums[w * CB : (w + 1) * CB, 0:128])
        plain = jnp.transpose(sums[w * CB : (w + 1) * CB, 128:256])
        even_sum = jnp.sum(jnp.where(odd == 0, plain, 0.0), axis=0, keepdims=True)
        odd_sum = jnp.sum(jnp.where(odd == 1, plain, 0.0), axis=0, keepdims=True)
        mean = jnp.sum(squares, axis=0, keepdims=True) + even_sum * odd_sum * (1.0 / 512)
        mean = 0.1 * jnp.maximum(mean, 0.0) + 1e-6
        level[:, w * CB : (w + 1) * CB] = jnp.broadcast_to(mean, (8, CB))

    greeted = N - 1 + jnp.where(chan > 0, 1, 0) + jnp.where(crossing, 3, 0) + jnp.where(relaying, 1, 0)
    pl.semaphore_wait(barrier, greeted)

    def first(s, d):
        p = partner(me, d)
        return pltpu.make_async_remote_copy(
            src_ref=send1.at[s, p], dst_ref=recv1.at[s, :, :, me], send_sem=s1_sem.at[s, d], recv_sem=r1_sem.at[s, d],
            device_id=(chan, p), device_id_type=MESH,
        )

    def first_own(s):
        return pltpu.make_async_copy(send1.at[s, me], recv1.at[s, :, :, me], l1_sem.at[s])

    def rim(s, g):
        return pltpu.make_async_remote_copy(
            src_ref=hsend.at[s, g], dst_ref=hrecv.at[s, g], send_sem=hs_sem.at[s, g], recv_sem=hr_sem.at[s, g],
            device_id=(chan - 1, me), device_id_type=MESH,
        )

    def to_relay(s, g):
        return pltpu.make_async_remote_copy(
            src_ref=hsend.at[s, g], dst_ref=passing.at[s], send_sem=hs_sem.at[s, g], recv_sem=pr_sem.at[s],
            device_id=(chan + g, me), device_id_type=MESH,
        )

    def from_relay(s):
        return pltpu.make_async_remote_copy(
            src_ref=passing.at[s], dst_ref=hrecv.at[s, y], send_sem=ps_sem.at[s], recv_sem=hr_sem.at[s, y],
            device_id=(chan - y - 1, me), device_id_type=MESH,
        )

    def second(s, d):
        p = partner(me, d)
        return pltpu.make_async_remote_copy(
            src_ref=send2.at[s, p], dst_ref=recv2.at[s, :, me], send_sem=s2_sem.at[s, d], recv_sem=r2_sem.at[s, d],
            device_id=(chan, p), device_id_type=MESH,
        )

    def second_own(s):
        return pltpu.make_async_copy(send2.at[s, me], recv2.at[s, :, me], l2_sem.at[s])

    def spectra(s, carry):
        pltpu.make_async_copy(tbl_hbm.at[s], tbl.at[s], tbl_sem.at[s]).wait()
        spec[...] = lax.dot_general(
            tbl[s], x_v[...], (((1,), (1,)), ((), ())), preferred_element_type=F32
        ).reshape(N, 2, FS, W4 * CB)

        def whiten(d, carry):
            p = partner(me, d)
            real, imag = spec[p, 0], spec[p, 1]
            scale = lax.rsqrt(real * real + imag * imag + level[0:1, :])
            for part, value in enumerate((real * scale, imag * scale)):
                for w in range(W4):
                    mix[pl.ds(part * 4 * FS + w, FS, stride=4), :] = value[:, w * CB : (w + 1) * CB]
            for part in range(2):
                rows = mix[part * 4 * FS : (part + 1) * 4 * FS, :]
                send1[s, p, part] = rows.astype(BF16).reshape(GS, 16, CB)

            @pl.when(d < N - 1)
            def _():
                first(s, d).start()

            return carry

        lax.fori_loop(0, N, whiten, 0)
        first_own(s).start()
        return carry

    lax.fori_loop(0, STAGES, spectra, 0)

    @pl.when(chan == N - 1)
    def _():
        hrecv[...] = jnp.zeros_like(hrecv)

    lane = lax.broadcasted_iota(jnp.int32, (8, CB), 1)
    shift = lane + 1
    sublane = lax.broadcasted_iota(jnp.int32, (8, CB), 0)
    in_own = (sublane + shift % 8) < 8

    def pick(bit, far, near):
        rows = near.shape[0]
        mask = (shift // bit) % 2 == 1
        return jnp.where(mask[None], far.reshape(rows // 8, 8, CB), near.reshape(rows // 8, 8, CB)).reshape(rows, CB)

    def skew(g):
        g = jnp.concatenate([pick(128, g[128:192], g[0:64]), g[64:192]], axis=0)
        g = pick(64, g[64:192], g[0:128])
        g = pick(32, g[32:128], g[0:96])
        g = pick(16, g[16:96], g[0:80])
        g = pick(8, g[8:80], g[0:72])
        g = g.reshape(9, 8, CB)
        for bit in (4, 2, 1):
            mask = (shift // bit) % 2 == 1
            g = jnp.where(mask[None], pltpu.roll(g, 8 - bit, axis=1), g)
        return jnp.where(in_own[None], g[0:8], g[1:9]).reshape(64, CB)

    def gather(s):
        for d in range(N - 1):
            first(s, d).wait_recv()
        first_own(s).wait()

        def pack(g, carry):
            left = recv1[s, 0, g].reshape(N * 16, CB)[:, 0:64]
            right = recv1[s, 1, g].reshape(N * 16, CB)[:, 0:64]
            hsend[s, g] = jnp.concatenate([left, right], axis=1)
            return carry

        lax.fori_loop(0, GS, pack, 0)

        @pl.when(chan > 0)
        def _():
            rim(s, 0).start()

        @pl.when(y > 0)
        def _():
            for g in range(1, GS):
                rim(s, g).start()

        @pl.when(crossing)
        def _():
            for g in range(1, GS):
                to_relay(s, g).start()

    def relay(s):
        @pl.when(relaying)
        def _():
            to_relay(s, 1).wait_recv()
            from_relay(s).start()

    def products(s):
        @pl.when(chan < N - 1)
        def _():
            for g in range(GS):
                rim(s, g).wait_recv()

        def group(g, carry):
            real = recv1[s, 0, g].reshape(N * 16, CB)
            imag = recv1[s, 1, g].reshape(N * 16, CB)
            rim_t = jnp.transpose(hrecv[s, g])
            real_t = jnp.concatenate([jnp.transpose(real), rim_t[0:64]], axis=0)
            imag_t = jnp.concatenate([jnp.transpose(imag), rim_t[64:128]], axis=0)
            right = jnp.concatenate(
                [jnp.concatenate([real, imag], axis=1), jnp.concatenate([imag, -real], axis=1)], axis=0
            )
            left = jnp.concatenate([real_t, imag_t], axis=1)
            which = (lax.broadcasted_iota(jnp.int32, left.shape, 1) % 16) // 4
            for f in range(4):
                gram[f * 192 : (f + 1) * 192, :] = jnp.dot(
                    jnp.where(which == f, left, jnp.zeros_like(left)), right, preferred_element_type=F32
                )
            for f in range(4):
                for part in range(2):
                    zbuf[pl.ds(part * FS + g * 4 + f, K, stride=2 * FS), :] = skew(
                        gram[f * 192 : (f + 1) * 192, part * CB : (part + 1) * CB]
                    )
            return carry

        lax.fori_loop(0, GS, group, 0)

        parity = lax.broadcasted_iota(jnp.int32, (4 * 2 * FS, CB), 0) % 2
        sign = jnp.where(parity == 0, 1.0 / 256, -1.0 / 256)

        def give(d, carry):
            p = partner(me, d)
            rows = zbuf[pl.ds(pl.multiple_of(p * 8 * FS, 8 * FS), 8 * FS), :]
            send2[s, p] = (rows * sign).astype(BF16).reshape(4, 2 * FS, CB)

            @pl.when(d < N - 1)
            def _():
                second(s, d).start()

            return carry

        lax.fori_loop(0, N, give, 0)
        second_own(s).start()

    gather(0)
    relay(0)

    def middle(s, carry):
        gather(s)
        relay(s)
        products(s - 1)
        return carry

    lax.fori_loop(1, STAGES, middle, 0)
    products(STAGES - 1)

    half = me // 8

    def lags(s, sides):
        for side in sides:
            for d in range(8 * side, min(8 * side + 8, N - 1)):
                second(s, d).wait_recv()
        if 1 in sides:
            second_own(s).wait()
        count = 8 * len(sides) * 2 * FS
        origin = 0 if len(sides) == 2 else (half if sides[0] == 1 else 1 - half) * 8
        origin = origin if len(sides) == 2 else pl.multiple_of(origin, 8)
        for k in range(4):
            block = recv2[s, k, pl.ds(origin, 8 * len(sides))].reshape(count, CB)
            lhs2[k * CB : (k + 1) * CB, 0:count] = jnp.transpose(block)

        def tile(t, carry):
            columns = pl.ds(pl.multiple_of(t * 512, 512), 512)
            rows = pl.ds(pl.multiple_of(origin * 2 * FS, 2 * FS), count)
            product = jnp.dot(lhs2[:, 0:count], tbl[s, rows, columns], preferred_element_type=F32)
            if s == 0:
                acc[t] = product
            elif sides != (0,):
                acc[t] += product
            else:
                o_ref[:, columns] = (acc[t] + product).astype(BF16)
            return carry

        lax.fori_loop(0, 4, tile, 0)

    for s in range(STAGES - 1):
        lags(s, (0, 1))
    lags(STAGES - 1, (1,))
    lags(STAGES - 1, (0,))

    for s in range(STAGES):
        for d in range(N - 1):
            first(s, d).wait_send()
            second(s, d).wait_send()

        @pl.when(chan > 0)
        def _():
            for g in range(GS):
                rim(s, g).wait_send()

        @pl.when(relaying)
        def _():
            from_relay(s).wait_send()


def per_device(traces, tbl):
    rows = W4 * CB
    dma = pltpu.SemaphoreType.DMA
    any_space = pl.BlockSpec(memory_space=pltpu.HBM)
    out = pl.pallas_call(
        kernel,
        out_shape=pltpu.VMEM((rows, S), BF16),
        in_specs=[any_space, any_space],
        out_specs=pl.BlockSpec(memory_space=pltpu.VMEM),
        scratch_shapes=[
            pltpu.VMEM((rows, S), BF16),
            pltpu.VMEM((STAGES, ROWS, S), BF16),
            pltpu.VMEM((rows, 256), F32),
            pltpu.VMEM((8, rows), F32),
            pltpu.VMEM((N, 2, FS, rows), F32),
            pltpu.VMEM((2 * 4 * FS, CB), F32),
            pltpu.VMEM((STAGES, N, 2, GS, 16, CB), BF16),
            pltpu.VMEM((STAGES, 2, GS, N, 16, CB), BF16),
            pltpu.VMEM((STAGES, GS, N * 16, CB), BF16),
            pltpu.VMEM((STAGES, GS, N * 16, CB), BF16),
            pltpu.VMEM((STAGES, N * 16, CB), BF16),
            pltpu.VMEM((4 * 192, 256), F32),
            pltpu.VMEM((K * 2 * FS, CB), F32),
            pltpu.VMEM((STAGES, N, 4, 2 * FS, CB), BF16),
            pltpu.VMEM((STAGES, 4, N, 2 * FS, CB), BF16),
            pltpu.VMEM((4 * CB, ROWS), BF16),
            pltpu.VMEM((4, rows, 512), F32),
            dma, dma((STAGES,)),
            dma((STAGES, N)), dma((STAGES, N)), dma((STAGES,)),
            dma((STAGES, GS)), dma((STAGES, GS)), dma((STAGES,)), dma((STAGES,)),
            dma((STAGES, N)), dma((STAGES, N)), dma((STAGES,)),
        ],
        compiler_params=pltpu.CompilerParams(collective_id=0, has_side_effects=True, vmem_limit_bytes=60 * 2**20),
        name="correlate",
    )(traces.reshape(rows, S), tbl)
    return out.reshape(traces.shape)


def solution(mesh):
    placed = P("freq", "chan", None)
    mapped = jax.shard_map(per_device, mesh=mesh, in_specs=(placed, P()), out_specs=placed, check_vma=False)
    return lambda traces: mapped(traces, jnp.asarray(table()))
```

```python
import functools
import math

import jax
import jax.numpy as jnp
import ml_dtypes
import numpy as np
from jax import lax
from jax.experimental import pallas as pl
from jax.experimental.pallas import tpu as pltpu
from jax.sharding import PartitionSpec as P

MESH = pl.DeviceIdType.MESH
BF16 = jnp.bfloat16
F32 = jnp.float32

S = 2048
W4 = 4
N = 16
CB = 128
K = 64
STAGES = 4
FS = 64 // STAGES
GS = FS // 4
ROWS = N * 2 * FS


def table():
    stage, shard, local = np.meshgrid(np.arange(STAGES), np.arange(N), np.arange(FS), indexing="ij")
    freq = (shard * 64 + stage * FS + local)[:, :, None, :, None]
    angle = (2.0 * math.pi / S) * ((freq * np.arange(S)) % S)
    values = np.concatenate([np.cos(angle), -np.sin(angle)], axis=2)
    return values.reshape(STAGES, ROWS, S).astype(ml_dtypes.bfloat16)


def partner(me, d):
    half, x, core = me // 8, (me // 2) % 4, me % 2
    half = (half + 1 - d // 8) % 2
    x = (x + 1 + (d % 8) // 2) % 4
    core = (core + 1 + d) % 2
    return half * 8 + x * 2 + core


def kernel(
    x_hbm, tbl_hbm, o_ref,
    x_v, tbl, sums, level, spec, mix, send1, recv1, hsend, hrecv, passing, gram, zbuf, send2, recv2, lhs2, acc,
    x_sem, tbl_sem, s1_sem, r1_sem, l1_sem, hs_sem, hr_sem, ps_sem, pr_sem, s2_sem, r2_sem, l2_sem,
):
    chan, me = lax.axis_index("chan"), lax.axis_index("freq")
    depth, y = chan // 4, chan % 4
    crossing = (y == 0) & (depth > 0)
    relaying = (y > 0) & (depth > 0)
    crossed = (y == 3) & (depth < 3)

    x_copy = pltpu.make_async_copy(x_hbm, x_v, x_sem)
    x_copy.start()
    tbl_copies = [pltpu.make_async_copy(tbl_hbm.at[s], tbl.at[s], tbl_sem.at[s]) for s in range(STAGES)]
    for copy in tbl_copies:
        copy.start()

    barrier = pltpu.get_barrier_semaphore()
    for d in range(N - 1):
        pl.semaphore_signal(barrier, inc=1, device_id=(chan, partner(me, d)), device_id_type=MESH)

    @pl.when(chan < N - 1)
    def _():
        pl.semaphore_signal(barrier, inc=1, device_id=(chan + 1, me), device_id_type=MESH)

    @pl.when(crossed)
    def _():
        for g in range(1, 4):
            pl.semaphore_signal(barrier, inc=1, device_id=(chan + 1 + g, me), device_id_type=MESH)

    @pl.when(relaying)
    def _():
        pl.semaphore_signal(barrier, inc=1, device_id=(chan - y, me), device_id_type=MESH)

    x_copy.wait()

    def fold(b, carry):
        rows = pl.ds(pl.multiple_of(b * 64, 64), 64)
        squares = jnp.zeros((64, 128), F32)
        plain = jnp.zeros((64, 128), F32)
        for i in range(S // 128):
            part = x_v[rows, i * 128 : (i + 1) * 128].astype(F32)
            squares += part * part
            plain += part
        sums[rows, 0:128] = squares
        sums[rows, 128:256] = plain
        return carry

    lax.fori_loop(0, W4 * CB // 64, fold, 0)
    odd = lax.broadcasted_iota(jnp.int32, (128, 128), 0) % 2
    for w in range(W4):
        squares = jnp.transpose(sums[w * CB : (w + 1) * CB, 0:128])
        plain = jnp.transpose(sums[w * CB : (w + 1) * CB, 128:256])
        even_sum = jnp.sum(jnp.where(odd == 0, plain, 0.0), axis=0, keepdims=True)
        odd_sum = jnp.sum(jnp.where(odd == 1, plain, 0.0), axis=0, keepdims=True)
        mean = jnp.sum(squares, axis=0, keepdims=True) + even_sum * odd_sum * (1.0 / 512)
        mean = 0.1 * jnp.maximum(mean, 0.0) + 1e-6
        level[:, w * CB : (w + 1) * CB] = jnp.broadcast_to(mean, (8, CB))

    greeted = N - 1 + jnp.where(chan > 0, 1, 0) + jnp.where(crossing, 3, 0) + jnp.where(relaying, 1, 0)
    pl.semaphore_wait(barrier, greeted)

    def first(s, d):
        p = partner(me, d)
        return pltpu.make_async_remote_copy(
            src_ref=send1.at[s, p], dst_ref=recv1.at[s, :, :, me], send_sem=s1_sem.at[s, d], recv_sem=r1_sem.at[s, d],
            device_id=(chan, p), device_id_type=MESH,
        )

    def first_own(s):
        return pltpu.make_async_copy(send1.at[s, me], recv1.at[s, :, :, me], l1_sem.at[s])

    def rim(s, g):
        return pltpu.make_async_remote_copy(
            src_ref=hsend.at[s, g], dst_ref=hrecv.at[s, g], send_sem=hs_sem.at[s, g], recv_sem=hr_sem.at[s, g],
            device_id=(chan - 1, me), device_id_type=MESH,
        )

    def to_relay(s, g):
        return pltpu.make_async_remote_copy(
            src_ref=hsend.at[s, g], dst_ref=passing.at[s], send_sem=hs_sem.at[s, g], recv_sem=pr_sem.at[s],
            device_id=(chan + g, me), device_id_type=MESH,
        )

    def from_relay(s):
        return pltpu.make_async_remote_copy(
            src_ref=passing.at[s], dst_ref=hrecv.at[s, y], send_sem=ps_sem.at[s], recv_sem=hr_sem.at[s, y],
            device_id=(chan - y - 1, me), device_id_type=MESH,
        )

    def second(s, d):
        p = partner(me, d)
        return pltpu.make_async_remote_copy(
            src_ref=send2.at[s, p], dst_ref=recv2.at[s, :, me], send_sem=s2_sem.at[s, d], recv_sem=r2_sem.at[s, d],
            device_id=(chan, p), device_id_type=MESH,
        )

    def second_own(s):
        return pltpu.make_async_copy(send2.at[s, me], recv2.at[s, :, me], l2_sem.at[s])

    def spectra(s, carry):
        pltpu.make_async_copy(tbl_hbm.at[s], tbl.at[s], tbl_sem.at[s]).wait()
        spec[...] = lax.dot_general(
            tbl[s], x_v[...], (((1,), (1,)), ((), ())), preferred_element_type=F32
        ).reshape(N, 2, FS, W4 * CB)

        def whiten(d, carry):
            p = partner(me, d)
            real, imag = spec[p, 0], spec[p, 1]
            scale = lax.rsqrt(real * real + imag * imag + level[0:1, :])
            for part, value in enumerate((real * scale, imag * scale)):
                for w in range(W4):
                    mix[pl.ds(part * 4 * FS + w, FS, stride=4), :] = value[:, w * CB : (w + 1) * CB]
            for part in range(2):
                rows = mix[part * 4 * FS : (part + 1) * 4 * FS, :]
                send1[s, p, part] = rows.astype(BF16).reshape(GS, 16, CB)

            @pl.when(d < N - 1)
            def _():
                first(s, d).start()

            return carry

        lax.fori_loop(0, N, whiten, 0)
        first_own(s).start()
        return carry

    lax.fori_loop(0, STAGES, spectra, 0)

    @pl.when(chan == N - 1)
    def _():
        hrecv[...] = jnp.zeros_like(hrecv)

    lane = lax.broadcasted_iota(jnp.int32, (8, CB), 1)
    shift = lane + 1
    sublane = lax.broadcasted_iota(jnp.int32, (8, CB), 0)
    in_own = (sublane + shift % 8) < 8

    def pick(bit, far, near):
        rows = near.shape[0]
        mask = (shift // bit) % 2 == 1
        return jnp.where(mask[None], far.reshape(rows // 8, 8, CB), near.reshape(rows // 8, 8, CB)).reshape(rows, CB)

    def skew(g):
        g = jnp.concatenate([pick(128, g[128:192], g[0:64]), g[64:192]], axis=0)
        g = pick(64, g[64:192], g[0:128])
        g = pick(32, g[32:128], g[0:96])
        g = pick(16, g[16:96], g[0:80])
        g = pick(8, g[8:80], g[0:72])
        g = g.reshape(9, 8, CB)
        for bit in (4, 2, 1):
            mask = (shift // bit) % 2 == 1
            g = jnp.where(mask[None], pltpu.roll(g, 8 - bit, axis=1), g)
        return jnp.where(in_own[None], g[0:8], g[1:9]).reshape(64, CB)

    def gather(s):
        for d in range(N - 1):
            first(s, d).wait_recv()
        first_own(s).wait()

        def pack(g, carry):
            left = recv1[s, 0, g].reshape(N * 16, CB)[:, 0:64]
            right = recv1[s, 1, g].reshape(N * 16, CB)[:, 0:64]
            hsend[s, g] = jnp.concatenate([left, right], axis=1)
            return carry

        lax.fori_loop(0, GS, pack, 0)

        @pl.when(chan > 0)
        def _():
            rim(s, 0).start()

        @pl.when(y > 0)
        def _():
            for g in range(1, GS):
                rim(s, g).start()

        @pl.when(crossing)
        def _():
            for g in range(1, GS):
                to_relay(s, g).start()

    def relay(s):
        @pl.when(relaying)
        def _():
            to_relay(s, 1).wait_recv()
            from_relay(s).start()

    def right_of(s, g):
        real = recv1[s, 0, g].reshape(N * 16, CB)
        imag = recv1[s, 1, g].reshape(N * 16, CB)
        right = jnp.concatenate(
            [jnp.concatenate([real, imag], axis=1), jnp.concatenate([imag, -real], axis=1)], axis=0
        )
        return real, imag, right

    def multiply(g, left, right, first_row):
        rows = left.shape[0]
        which = (lax.broadcasted_iota(jnp.int32, left.shape, 1) % 16) // 4
        for f in range(4):
            gram[g, f * 192 + first_row : f * 192 + first_row + rows, :] = jnp.dot(
                jnp.where(which == f, left, jnp.zeros_like(left)), right, preferred_element_type=F32
            )

    def products(s):
        def own(g, carry):
            real, imag, right = right_of(s, g)
            multiply(g, jnp.concatenate([jnp.transpose(real), jnp.transpose(imag)], axis=1), right, 0)
            return carry

        lax.fori_loop(0, GS, own, 0)

        @pl.when(chan < N - 1)
        def _():
            for g in range(GS):
                rim(s, g).wait_recv()

        def group(g, carry):
            right = right_of(s, g)[2]
            rim_t = jnp.transpose(hrecv[s, g])
            multiply(g, jnp.concatenate([rim_t[0:64], rim_t[64:128]], axis=1), right, 128)
            for f in range(4):
                for part in range(2):
                    zbuf[pl.ds(part * FS + g * 4 + f, K, stride=2 * FS), :] = skew(
                        gram[g, f * 192 : (f + 1) * 192, part * CB : (part + 1) * CB]
                    )
            return carry

        lax.fori_loop(0, GS, group, 0)

        parity = lax.broadcasted_iota(jnp.int32, (4 * 2 * FS, CB), 0) % 2
        sign = jnp.where(parity == 0, 1.0 / 256, -1.0 / 256)

        def give(i, carry):
            d = (i % 2) * 8 + i // 2
            p = partner(me, d)
            rows = zbuf[pl.ds(pl.multiple_of(p * 8 * FS, 8 * FS), 8 * FS), :]
            send2[s, p] = (rows * sign).astype(BF16).reshape(4, 2 * FS, CB)

            @pl.when(d < N - 1)
            def _():
                second(s, d).start()

            return carry

        lax.fori_loop(0, N, give, 0)
        second_own(s).start()

    gather(0)
    relay(0)

    def middle(s, carry):
        gather(s)
        relay(s)
        products(s - 1)
        return carry

    lax.fori_loop(1, STAGES, middle, 0)
    products(STAGES - 1)

    half = me // 8

    def lags(s, sides):
        for side in sides:
            for d in range(8 * side, min(8 * side + 8, N - 1)):
                second(s, d).wait_recv()
        if 1 in sides:
            second_own(s).wait()
        count = 8 * len(sides) * 2 * FS
        origin = 0 if len(sides) == 2 else (half if sides[0] == 1 else 1 - half) * 8
        origin = origin if len(sides) == 2 else pl.multiple_of(origin, 8)
        for k in range(4):
            block = recv2[s, k, pl.ds(origin, 8 * len(sides))].reshape(count, CB)
            lhs2[k * CB : (k + 1) * CB, 0:count] = jnp.transpose(block)

        def tile(t, carry):
            columns = pl.ds(pl.multiple_of(t * 512, 512), 512)
            rows = pl.ds(pl.multiple_of(origin * 2 * FS, 2 * FS), count)
            product = jnp.dot(lhs2[:, 0:count], tbl[s, rows, columns], preferred_element_type=F32)
            if s == 0:
                acc[t] = product
            elif sides != (0,):
                acc[t] += product
            else:
                o_ref[:, columns] = (acc[t] + product).astype(BF16)
            return carry

        lax.fori_loop(0, 4, tile, 0)

    for s in range(STAGES - 1):
        lags(s, (0, 1))
    lags(STAGES - 1, (1,))
    lags(STAGES - 1, (0,))

    for s in range(STAGES):
        for d in range(N - 1):
            first(s, d).wait_send()
            second(s, d).wait_send()

        @pl.when(chan > 0)
        def _():
            for g in range(GS):
                rim(s, g).wait_send()

        @pl.when(relaying)
        def _():
            from_relay(s).wait_send()


def per_device(traces, tbl):
    rows = W4 * CB
    dma = pltpu.SemaphoreType.DMA
    any_space = pl.BlockSpec(memory_space=pltpu.HBM)
    out = pl.pallas_call(
        kernel,
        out_shape=pltpu.VMEM((rows, S), BF16),
        in_specs=[any_space, any_space],
        out_specs=pl.BlockSpec(memory_space=pltpu.VMEM),
        scratch_shapes=[
            pltpu.VMEM((rows, S), BF16),
            pltpu.VMEM((STAGES, ROWS, S), BF16),
            pltpu.VMEM((rows, 256), F32),
            pltpu.VMEM((8, rows), F32),
            pltpu.VMEM((N, 2, FS, rows), F32),
            pltpu.VMEM((2 * 4 * FS, CB), F32),
            pltpu.VMEM((STAGES, N, 2, GS, 16, CB), BF16),
            pltpu.VMEM((STAGES, 2, GS, N, 16, CB), BF16),
            pltpu.VMEM((STAGES, GS, N * 16, CB), BF16),
            pltpu.VMEM((STAGES, GS, N * 16, CB), BF16),
            pltpu.VMEM((STAGES, N * 16, CB), BF16),
            pltpu.VMEM((GS, 4 * 192, 256), F32),
            pltpu.VMEM((K * 2 * FS, CB), F32),
            pltpu.VMEM((STAGES, N, 4, 2 * FS, CB), BF16),
            pltpu.VMEM((STAGES, 4, N, 2 * FS, CB), BF16),
            pltpu.VMEM((4 * CB, ROWS), BF16),
            pltpu.VMEM((4, rows, 512), F32),
            dma, dma((STAGES,)),
            dma((STAGES, N)), dma((STAGES, N)), dma((STAGES,)),
            dma((STAGES, GS)), dma((STAGES, GS)), dma((STAGES,)), dma((STAGES,)),
            dma((STAGES, N)), dma((STAGES, N)), dma((STAGES,)),
        ],
        compiler_params=pltpu.CompilerParams(collective_id=0, has_side_effects=True, vmem_limit_bytes=60 * 2**20),
        name="correlate",
    )(traces.reshape(rows, S), tbl)
    return out.reshape(traces.shape)


def solution(mesh):
    placed = P("freq", "chan", None)
    mapped = jax.shard_map(per_device, mesh=mesh, in_specs=(placed, P()), out_specs=placed, check_vma=False)
    return lambda traces: mapped(traces, jnp.asarray(table()))
```

```python
import functools
import math

import jax
import jax.numpy as jnp
import ml_dtypes
import numpy as np
from jax import lax
from jax.experimental import pallas as pl
from jax.experimental.pallas import tpu as pltpu
from jax.sharding import PartitionSpec as P

MESH = pl.DeviceIdType.MESH
BF16 = jnp.bfloat16
F32 = jnp.float32

S = 2048
W4 = 4
N = 16
CB = 128
K = 64
STAGES = 4
FS = 64 // STAGES
GS = FS // 4
ROWS = N * 2 * FS


def table():
    stage, shard, local = np.meshgrid(np.arange(STAGES), np.arange(N), np.arange(FS), indexing="ij")
    freq = (shard * 64 + stage * FS + local)[:, :, None, :, None]
    angle = (2.0 * math.pi / S) * ((freq * np.arange(S)) % S)
    values = np.concatenate([np.cos(angle), -np.sin(angle)], axis=2)
    return values.reshape(STAGES, ROWS, S).astype(ml_dtypes.bfloat16)


def partner(me, d):
    half, x, core = me // 8, (me // 2) % 4, me % 2
    half = (half + 1 - d // 8) % 2
    x = (x + 1 + (d % 8) // 2) % 4
    core = (core + 1 + d) % 2
    return half * 8 + x * 2 + core


def kernel(
    x_hbm, tbl_hbm, o_ref,
    x_v, tbl, sums, level, spec, mix, send1, recv1, hsend, hrecv, passing, gram, zbuf, send2, recv2, lhs2, acc,
    x_sem, tbl_sem, s1_sem, r1_sem, l1_sem, hs_sem, hr_sem, ps_sem, pr_sem, s2_sem, r2_sem, l2_sem,
):
    chan, me = lax.axis_index("chan"), lax.axis_index("freq")
    depth, y = chan // 4, chan % 4
    crossing = (y == 0) & (depth > 0)
    relaying = (y > 0) & (depth > 0)
    crossed = (y == 3) & (depth < 3)

    x_copy = pltpu.make_async_copy(x_hbm, x_v, x_sem)
    x_copy.start()
    tbl_copies = [pltpu.make_async_copy(tbl_hbm.at[s], tbl.at[s], tbl_sem.at[s]) for s in range(STAGES)]
    for copy in tbl_copies:
        copy.start()

    barrier = pltpu.get_barrier_semaphore()
    for d in range(N - 1):
        pl.semaphore_signal(barrier, inc=1, device_id=(chan, partner(me, d)), device_id_type=MESH)

    @pl.when(chan < N - 1)
    def _():
        pl.semaphore_signal(barrier, inc=1, device_id=(chan + 1, me), device_id_type=MESH)

    @pl.when(crossed)
    def _():
        for g in range(1, 4):
            pl.semaphore_signal(barrier, inc=1, device_id=(chan + 1 + g, me), device_id_type=MESH)

    @pl.when(relaying)
    def _():
        pl.semaphore_signal(barrier, inc=1, device_id=(chan - y, me), device_id_type=MESH)

    x_copy.wait()

    def fold(b, carry):
        rows = pl.ds(pl.multiple_of(b * 64, 64), 64)
        squares = jnp.zeros((64, 128), F32)
        plain = jnp.zeros((64, 128), F32)
        for i in range(S // 128):
            part = x_v[rows, i * 128 : (i + 1) * 128].astype(F32)
            squares += part * part
            plain += part
        sums[rows, 0:128] = squares
        sums[rows, 128:256] = plain
        return carry

    lax.fori_loop(0, W4 * CB // 64, fold, 0)
    odd = lax.broadcasted_iota(jnp.int32, (128, 128), 0) % 2
    for w in range(W4):
        squares = jnp.transpose(sums[w * CB : (w + 1) * CB, 0:128])
        plain = jnp.transpose(sums[w * CB : (w + 1) * CB, 128:256])
        even_sum = jnp.sum(jnp.where(odd == 0, plain, 0.0), axis=0, keepdims=True)
        odd_sum = jnp.sum(jnp.where(odd == 1, plain, 0.0), axis=0, keepdims=True)
        mean = jnp.sum(squares, axis=0, keepdims=True) + even_sum * odd_sum * (1.0 / 512)
        mean = 0.1 * jnp.maximum(mean, 0.0) + 1e-6
        level[:, w * CB : (w + 1) * CB] = jnp.broadcast_to(mean, (8, CB))

    greeted = N - 1 + jnp.where(chan > 0, 1, 0) + jnp.where(crossing, 3, 0) + jnp.where(relaying, 1, 0)
    pl.semaphore_wait(barrier, greeted)

    def first(s, d):
        p = partner(me, d)
        return pltpu.make_async_remote_copy(
            src_ref=send1.at[s, p], dst_ref=recv1.at[s, :, :, me], send_sem=s1_sem.at[s, d], recv_sem=r1_sem.at[s, d],
            device_id=(chan, p), device_id_type=MESH,
        )

    def first_own(s):
        return pltpu.make_async_copy(send1.at[s, me], recv1.at[s, :, :, me], l1_sem.at[s])

    def rim(s, g):
        return pltpu.make_async_remote_copy(
            src_ref=hsend.at[s, g], dst_ref=hrecv.at[s, g], send_sem=hs_sem.at[s, g], recv_sem=hr_sem.at[s, g],
            device_id=(chan - 1, me), device_id_type=MESH,
        )

    def to_relay(s, g):
        return pltpu.make_async_remote_copy(
            src_ref=hsend.at[s, g], dst_ref=passing.at[s], send_sem=hs_sem.at[s, g], recv_sem=pr_sem.at[s],
            device_id=(chan + g, me), device_id_type=MESH,
        )

    def from_relay(s):
        return pltpu.make_async_remote_copy(
            src_ref=passing.at[s], dst_ref=hrecv.at[s, y], send_sem=ps_sem.at[s], recv_sem=hr_sem.at[s, y],
            device_id=(chan - y - 1, me), device_id_type=MESH,
        )

    def second(s, d):
        p = partner(me, d)
        return pltpu.make_async_remote_copy(
            src_ref=send2.at[s, p], dst_ref=recv2.at[s, :, me], send_sem=s2_sem.at[s, d], recv_sem=r2_sem.at[s, d],
            device_id=(chan, p), device_id_type=MESH,
        )

    def second_own(s):
        return pltpu.make_async_copy(send2.at[s, me], recv2.at[s, :, me], l2_sem.at[s])

    def spectra(s, carry):
        pltpu.make_async_copy(tbl_hbm.at[s], tbl.at[s], tbl_sem.at[s]).wait()
        spec[...] = lax.dot_general(
            tbl[s], x_v[...], (((1,), (1,)), ((), ())), preferred_element_type=F32
        ).reshape(N, 2, FS, W4 * CB)

        def whiten(d, carry):
            p = partner(me, d)
            real, imag = spec[p, 0], spec[p, 1]
            scale = lax.rsqrt(real * real + imag * imag + level[0:1, :])
            for part, value in enumerate((real * scale, imag * scale)):
                for w in range(W4):
                    mix[pl.ds(part * 4 * FS + w, FS, stride=4), :] = value[:, w * CB : (w + 1) * CB]
            for part in range(2):
                rows = mix[part * 4 * FS : (part + 1) * 4 * FS, :]
                send1[s, p, part] = rows.astype(BF16).reshape(GS, 16, CB)

            @pl.when(d < N - 1)
            def _():
                first(s, d).start()

            return carry

        lax.fori_loop(0, N, whiten, 0)
        first_own(s).start()
        return carry

    lax.fori_loop(0, STAGES, spectra, 0)

    @pl.when(chan == N - 1)
    def _():
        hrecv[...] = jnp.zeros_like(hrecv)

    lane = lax.broadcasted_iota(jnp.int32, (8, CB), 1)
    shift = lane + 1
    sublane = lax.broadcasted_iota(jnp.int32, (8, CB), 0)
    in_own = (sublane + shift % 8) < 8

    def pick(bit, far, near):
        rows = near.shape[0]
        mask = (shift // bit) % 2 == 1
        return jnp.where(mask[None], far.reshape(rows // 8, 8, CB), near.reshape(rows // 8, 8, CB)).reshape(rows, CB)

    def skew(g):
        g = jnp.concatenate([pick(128, g[128:192], g[0:64]), g[64:192]], axis=0)
        g = pick(64, g[64:192], g[0:128])
        g = pick(32, g[32:128], g[0:96])
        g = pick(16, g[16:96], g[0:80])
        g = pick(8, g[8:80], g[0:72])
        g = g.reshape(9, 8, CB)
        for bit in (4, 2, 1):
            mask = (shift // bit) % 2 == 1
            g = jnp.where(mask[None], pltpu.roll(g, 8 - bit, axis=1), g)
        return jnp.where(in_own[None], g[0:8], g[1:9]).reshape(64, CB)

    def gather(s):
        for d in range(N - 1):
            first(s, d).wait_recv()
        first_own(s).wait()

        def pack(g, carry):
            left = recv1[s, 0, g].reshape(N * 16, CB)[:, 0:64]
            right = recv1[s, 1, g].reshape(N * 16, CB)[:, 0:64]
            hsend[s, g] = jnp.concatenate([left, right], axis=1)
            return carry

        lax.fori_loop(0, GS, pack, 0)

        @pl.when(chan > 0)
        def _():
            rim(s, 0).start()

        @pl.when(y > 0)
        def _():
            for g in range(1, GS):
                rim(s, g).start()

        @pl.when(crossing)
        def _():
            for g in range(1, GS):
                to_relay(s, g).start()

    def relay(s):
        @pl.when(relaying)
        def _():
            to_relay(s, 1).wait_recv()
            from_relay(s).start()

    def products(s):
        @pl.when(chan < N - 1)
        def _():
            for g in range(GS):
                rim(s, g).wait_recv()

        def group(g, carry):
            real = recv1[s, 0, g].reshape(N * 16, CB)
            imag = recv1[s, 1, g].reshape(N * 16, CB)
            rim_t = jnp.transpose(hrecv[s, g])
            real_t = jnp.concatenate([jnp.transpose(real), rim_t[0:64]], axis=0)
            imag_t = jnp.concatenate([jnp.transpose(imag), rim_t[64:128]], axis=0)
            right = jnp.concatenate(
                [jnp.concatenate([real, imag], axis=1), jnp.concatenate([imag, -real], axis=1)], axis=0
            )
            left = jnp.concatenate([real_t, imag_t], axis=1)
            which = (lax.broadcasted_iota(jnp.int32, left.shape, 1) % 16) // 4
            for f in range(4):
                gram[f * 192 : (f + 1) * 192, :] = jnp.dot(
                    jnp.where(which == f, left, jnp.zeros_like(left)), right, preferred_element_type=F32
                )
            for f in range(4):
                for part in range(2):
                    zbuf[pl.ds(part * FS + g * 4 + f, K, stride=2 * FS), :] = skew(
                        gram[f * 192 : (f + 1) * 192, part * CB : (part + 1) * CB]
                    )
            return carry

        lax.fori_loop(0, GS, group, 0)

        parity = lax.broadcasted_iota(jnp.int32, (4 * 2 * FS, CB), 0) % 2
        sign = jnp.where(parity == 0, 1.0 / 256, -1.0 / 256)

        def give(d, carry):
            p = partner(me, d)
            rows = zbuf[pl.ds(pl.multiple_of(p * 8 * FS, 8 * FS), 8 * FS), :]
            send2[s, p] = (rows * sign).astype(BF16).reshape(4, 2 * FS, CB)

            @pl.when(d < N - 1)
            def _():
                second(s, d).start()

            return carry

        lax.fori_loop(0, N, give, 0)
        second_own(s).start()

    gather(0)
    relay(0)

    def middle(s, carry):
        gather(s)
        relay(s)
        products(s - 1)
        return carry

    lax.fori_loop(1, STAGES, middle, 0)
    half = me // 8

    def lags(s, sides):
        for side in sides:
            for d in range(8 * side, min(8 * side + 8, N - 1)):
                second(s, d).wait_recv()
        if 1 in sides:
            second_own(s).wait()
        count = 8 * len(sides) * 2 * FS
        origin = 0 if len(sides) == 2 else (half if sides[0] == 1 else 1 - half) * 8
        origin = origin if len(sides) == 2 else pl.multiple_of(origin, 8)
        for k in range(4):
            block = recv2[s, k, pl.ds(origin, 8 * len(sides))].reshape(count, CB)
            lhs2[k * CB : (k + 1) * CB, 0:count] = jnp.transpose(block)

        def tile(t, carry):
            columns = pl.ds(pl.multiple_of(t * 512, 512), 512)
            rows = pl.ds(pl.multiple_of(origin * 2 * FS, 2 * FS), count)
            product = jnp.dot(lhs2[:, 0:count], tbl[s, rows, columns], preferred_element_type=F32)
            if s == 0:
                acc[t] = product
            elif sides != (0,):
                acc[t] += product
            else:
                o_ref[:, columns] = (acc[t] + product).astype(BF16)
            return carry

        lax.fori_loop(0, 4, tile, 0)

    for s in range(1):
        lags(s, (0, 1))
    products(STAGES - 1)

    for s in range(1, STAGES - 1):
        lags(s, (0, 1))
    lags(STAGES - 1, (1,))
    lags(STAGES - 1, (0,))

    for s in range(STAGES):
        for d in range(N - 1):
            first(s, d).wait_send()
            second(s, d).wait_send()

        @pl.when(chan > 0)
        def _():
            for g in range(GS):
                rim(s, g).wait_send()

        @pl.when(relaying)
        def _():
            from_relay(s).wait_send()


def per_device(traces, tbl):
    rows = W4 * CB
    dma = pltpu.SemaphoreType.DMA
    any_space = pl.BlockSpec(memory_space=pltpu.HBM)
    out = pl.pallas_call(
        kernel,
        out_shape=pltpu.VMEM((rows, S), BF16),
        in_specs=[any_space, any_space],
        out_specs=pl.BlockSpec(memory_space=pltpu.VMEM),
        scratch_shapes=[
            pltpu.VMEM((rows, S), BF16),
            pltpu.VMEM((STAGES, ROWS, S), BF16),
            pltpu.VMEM((rows, 256), F32),
            pltpu.VMEM((8, rows), F32),
            pltpu.VMEM((N, 2, FS, rows), F32),
            pltpu.VMEM((2 * 4 * FS, CB), F32),
            pltpu.VMEM((STAGES, N, 2, GS, 16, CB), BF16),
            pltpu.VMEM((STAGES, 2, GS, N, 16, CB), BF16),
            pltpu.VMEM((STAGES, GS, N * 16, CB), BF16),
            pltpu.VMEM((STAGES, GS, N * 16, CB), BF16),
            pltpu.VMEM((STAGES, N * 16, CB), BF16),
            pltpu.VMEM((4 * 192, 256), F32),
            pltpu.VMEM((K * 2 * FS, CB), F32),
            pltpu.VMEM((STAGES, N, 4, 2 * FS, CB), BF16),
            pltpu.VMEM((STAGES, 4, N, 2 * FS, CB), BF16),
            pltpu.VMEM((4 * CB, ROWS), BF16),
            pltpu.VMEM((4, rows, 512), F32),
            dma, dma((STAGES,)),
            dma((STAGES, N)), dma((STAGES, N)), dma((STAGES,)),
            dma((STAGES, GS)), dma((STAGES, GS)), dma((STAGES,)), dma((STAGES,)),
            dma((STAGES, N)), dma((STAGES, N)), dma((STAGES,)),
        ],
        compiler_params=pltpu.CompilerParams(collective_id=0, has_side_effects=True, vmem_limit_bytes=60 * 2**20),
        name="correlate",
    )(traces.reshape(rows, S), tbl)
    return out.reshape(traces.shape)


def solution(mesh):
    placed = P("freq", "chan", None)
    mapped = jax.shard_map(per_device, mesh=mesh, in_specs=(placed, P()), out_specs=placed, check_vma=False)
    return lambda traces: mapped(traces, jnp.asarray(table()))
```
